32 devices in a mesh: prow: 4 (over z), pcol: 8 (over y, x, core).
Axes of the slice: x: 2, y: 2, z: 4, core: 2. Of those that a mesh axis runs over, the one named last changes fastest.
Arguments:
- matrix: bfloat16 [8, 4, 5, 8, 256, 256], P(None, 'prow', None, 'pcol'), may hold values from -6 to 6
- lower_inverse: bfloat16 [4, 256, 256], replicated
- upper_inverse: bfloat16 [4, 256, 256], replicated
- row_first: int32 [8, 4], P(None, 'prow'), may hold values from 0 to 4, as said below
- col_mask: int32 [4, 5, 8], P(None, None, 'pcol'), may hold values from 0 to 1, as said below
Outputs:
- factored: bfloat16 [8, 4, 5, 8, 256, 256], P(None, 'prow', None, 'pcol')
The draws below stay inside these ranges and needn't reach their ends.
Inputs may be any that keep to these rules, and one draw needn't show every extreme that they name: `row_first`: 4 means no panel; tile rows below 4 take 4. `col_mask`: 0 for tile columns j <= k, 1 for k < j < 4.
All inputs are finite; a program needn't handle non-finite values.
Results may differ from the reference program's by a relative error of at most 0.007.
Values may be sent and summed in bfloat16 or wider, within the bound.
No kernel may reach another device: no remote copies, remote signals or barrier semaphores. Data moves between devices by JAX's collectives and lax.ppermute only.
A program may use at most 128 MiB of HBM per device.

```python
import math
import jax
import jax.numpy as jnp
from jax import lax

B = 256
K = 4
RT = 8
CT = 5
N_PROW = 4
N_PCOL = 8


def draw_lower_inverse(key, part):
    entries = jax.random.normal(key, (K, B, B), jnp.float32)
    strict = jnp.tril(entries, -1) * (0.5 / math.sqrt(B))
    return (strict + jnp.eye(B, dtype=jnp.float32)).astype(jnp.bfloat16)


def draw_upper_inverse(key, part):
    key_rate = jax.random.fold_in(key, 11)
    key_entry = jax.random.fold_in(key, 12)
    diagonal = jnp.exp(jax.random.uniform(key_rate, (K, B), jnp.float32, math.log(1.0 / 32.0), math.log(1.0 / 8.0)))
    entries = jax.random.normal(key_entry, (K, B, B), jnp.float32)
    strict = jnp.triu(entries, 1) * (0.5 / (16.0 * math.sqrt(B)))
    return (strict + diagonal[:, :, None] * jnp.eye(B, dtype=jnp.float32)).astype(jnp.bfloat16)


def draw_row_first(key, part):
    drawn = jax.random.randint(key, (RT, N_PROW), 0, K + 1)
    tile_index = jnp.arange(RT)[:, None] * N_PROW + jnp.arange(N_PROW)[None, :]
    return jnp.where(tile_index < K, K, drawn).astype(jnp.int32)


def draw_col_mask(key, part):
    key_rate = jax.random.fold_in(key, 21)
    key_coin = jax.random.fold_in(key, 22)
    density = jax.random.randint(key_rate, (N_PCOL,), 1, 9)
    coin_bits = jax.random.randint(key_coin, (K, CT, N_PCOL), 0, 8)
    present = (coin_bits < density[None, None, :]).astype(jnp.int32)
    tile_index = jnp.arange(CT)[:, None] * N_PCOL + jnp.arange(N_PCOL)[None, :]
    panel_index = jnp.arange(K)[:, None, None]
    return jnp.where(tile_index[None] <= panel_index, 0, jnp.where(tile_index[None] < K, 1, present)).astype(jnp.int32)


def block_scale(key, shape, cuts, least, largest):
    def one(dim, parts):
        steps = jax.random.uniform(jax.random.fold_in(jax.random.fold_in(key, 6), dim), (parts,), jnp.float32, least / len(cuts), largest / len(cuts))
        return jnp.repeat(jnp.exp(steps), shape[dim] // parts).reshape((-1,) + (1,) * (len(shape) - dim - 1))

    gain = one(*cuts[0])
    for cut in cuts[1:]:
        gain = gain * one(*cut)
    return gain


def gaussian(stream_key, extent, deviation, reach, pieces=(), held_as=jnp.bfloat16):
    values = jax.random.normal(stream_key, extent, jnp.float32) * deviation
    if len(pieces) > 0:
        values = block_scale(stream_key, extent, pieces, -0.22, 0.18) * values
    return jnp.clip(values, min=-reach, max=reach).astype(held_as)


def setup_inputs(seed: int = 0) -> dict:
    keys = jax.random.split(jax.random.key(seed), 6)
    matrix = gaussian(keys[0], (RT, N_PROW, CT, N_PCOL, B, B), 1.0, 6.0, ((1, 4), (3, 8)))
    lower_inverse = draw_lower_inverse(jax.random.fold_in(keys[5], 71), 0)
    upper_inverse = draw_upper_inverse(jax.random.fold_in(keys[5], 71), 0)
    row_first = draw_row_first(jax.random.fold_in(keys[5], 71), 0)
    col_mask = draw_col_mask(jax.random.fold_in(keys[5], 71), 0)
    return dict(matrix=matrix, lower_inverse=lower_inverse, upper_inverse=upper_inverse, row_first=row_first, col_mask=col_mask)


def reference(matrix, lower_inverse, upper_inverse, row_first, col_mask):
    tile_rows = RT * N_PROW
    tile_cols = CT * N_PCOL
    running = matrix.reshape(tile_rows, tile_cols, B, B).astype(jnp.float32)
    first_flat = row_first.reshape(tile_rows)
    col_flat = col_mask.reshape(K, tile_cols)
    lowers = []
    uppers = []
    for panel in range(K):
        lower_panel = jnp.einsum("rab,bc->rac", running[:, panel], upper_inverse[panel].astype(jnp.float32), precision=lax.Precision.HIGHEST)
        lower_panel = jnp.where((first_flat <= panel)[:, None, None], lower_panel, 0.0).astype(jnp.bfloat16)
        upper_panel = jnp.einsum("ab,jbc->jac", lower_inverse[panel].astype(jnp.float32), running[panel], precision=lax.Precision.HIGHEST)
        upper_panel = jnp.where((col_flat[panel] == 1)[:, None, None], upper_panel, 0.0).astype(jnp.bfloat16)
        upper_wide = upper_panel.astype(jnp.float32)

        def update_row(triple):
            tile_row, lower_tile, active = triple
            return lax.cond(active, lambda: tile_row - jnp.einsum("ab,jbc->jac", lower_tile.astype(jnp.float32), upper_wide, precision=lax.Precision.HIGHEST), lambda: tile_row)

        running = lax.map(update_row, (running, lower_panel, first_flat <= panel))
        lowers.append(lower_panel)
        uppers.append(upper_panel)
    result = running.astype(jnp.bfloat16)
    result = result.at[:, :K].set(jnp.transpose(jnp.stack(lowers), (1, 0, 2, 3)))
    result = result.at[:K].set(jnp.stack(uppers))
    return result.reshape(RT, N_PROW, CT, N_PCOL, B, B)
```

```python
import functools

import jax
import jax.numpy as jnp
from jax import lax
from jax.experimental import pallas as pl
from jax.experimental.pallas import tpu as pltpu
from jax.sharding import PartitionSpec as P

F32 = jnp.float32
BF16 = jnp.bfloat16
VMEM_BYTES = 58 * 1024 * 1024
IN_VMEM = pl.BlockSpec(memory_space=pltpu.VMEM)
IN_SMEM = pl.BlockSpec(memory_space=pltpu.SMEM)


def dot(a, b):
    return jnp.dot(a, b, preferred_element_type=F32)


def params():
    return pltpu.CompilerParams(vmem_limit_bytes=VMEM_BYTES)


def head_kernel(panels, index, inverse, *refs):
    pieces, out = refs[:-1], refs[-1]
    for r, piece in enumerate(pieces):
        k = index[r]

        @pl.when(k < panels - 1)
        def _():
            out[k] = dot(inverse[k], piece[0]).astype(BF16)


def head(panels, index, inverse, pieces):
    tile = inverse.shape[1]
    return pl.pallas_call(
        functools.partial(head_kernel, panels),
        out_shape=jax.ShapeDtypeStruct((panels - 1, tile, tile), BF16),
        in_specs=[IN_SMEM] + [IN_VMEM] * (1 + len(pieces)),
        out_specs=IN_VMEM,
        compiler_params=params(),
    )(index, inverse, *pieces)


def lower_kernel(panels, parts, slot, row_first, inverse, *refs):
    columns, heads = refs[:parts], refs[parts : 2 * parts]
    out, raw, top, sem = refs[2 * parts :]
    rows, tile = raw.shape[1], raw.shape[3]
    per = panels // parts
    copies = []
    for i in range(parts):
        for j in range(per):
            k = slot[i * per + j]
            copies.append(pltpu.make_async_copy(columns[i].at[j], raw.at[k], sem.at[0, i * per + j]))
            copies.append(pltpu.make_async_copy(heads[i].at[j], top.at[k], sem.at[1, i * per + j]))
    for copy in copies:
        copy.start()
    for copy in copies:
        copy.wait()
    for k in range(panels):
        s = raw[k].reshape(rows * tile, tile)
        if k == 0:
            solved = dot(s, inverse[0])
        else:
            known = out[:, : k * tile]
            upper = top[k, :k].reshape(k * tile, tile)
            s = s.astype(F32) - dot(known, upper)
            high = s.astype(BF16)
            low = (s - high.astype(F32)).astype(BF16)
            solved = dot(high, inverse[k]) + dot(low, inverse[k])
        for a in range(rows):
            live = row_first[a] <= k
            block = solved[a * tile : (a + 1) * tile]
            out[a * tile : (a + 1) * tile, k * tile : (k + 1) * tile] = jnp.where(live, block, 0.0).astype(BF16)


def lower(panels, slot, row_first, inverse, columns, heads):
    parts = len(columns)
    rows, tile = columns[0].shape[1], columns[0].shape[2]
    any_space = pl.BlockSpec(memory_space=pl.ANY)
    return pl.pallas_call(
        functools.partial(lower_kernel, panels, parts),
        out_shape=jax.ShapeDtypeStruct((rows * tile, panels * tile), BF16),
        in_specs=[IN_SMEM, IN_SMEM, IN_VMEM] + [any_space] * (2 * parts),
        out_specs=IN_VMEM,
        scratch_shapes=[
            pltpu.VMEM((panels, rows, tile, tile), BF16),
            pltpu.VMEM((panels, panels - 1, tile, tile), BF16),
            pltpu.SemaphoreType.DMA((2, panels)),
        ],
        compiler_params=params(),
    )(slot, row_first, inverse, *columns, *heads)


def update_kernel(panels, skip, start, index, place, mask, inverse, lowers, *refs):
    pieces = refs[: len(refs) - 3 - (1 if start else 0)]
    matrix, out, upper = refs[len(pieces)], refs[-2], refs[-1]
    step = pl.program_id(0)
    c = step + start
    tile = inverse.shape[1]
    rows = lowers.shape[0] // tile
    row_at, column_at = place[0], place[1]
    for r, piece in enumerate(pieces):
        k = index[r]
        solved = dot(inverse[k], piece[step])
        live = mask[k, c] == 1
        upper[pl.ds(pl.multiple_of(k * tile, tile), tile), :] = jnp.where(live, solved, 0.0).astype(BF16)
    own = pl.ds(pl.multiple_of(jnp.minimum(row_at, panels - 1) * tile, tile), tile)
    for a in range(rows):
        s = matrix[a + skip, 0].astype(F32) - dot(lowers[a * tile : (a + 1) * tile, :], upper[...])
        out[a + skip, 0] = s.astype(BF16)
    if start == 0:

        @pl.when((step == 0) & (column_at < panels))
        def _():
            for k in range(panels):

                @pl.when(column_at == k)
                def _():
                    for a in range(rows):
                        out[a + skip, 0] = lowers[a * tile : (a + 1) * tile, k * tile : (k + 1) * tile]

    @pl.when(row_at < panels)
    def _():
        out[0, 0] = upper[own, :]


def update(panels, skip, start, index, place, mask, inverse, lowers, pieces, matrix, so_far):
    tile = inverse.shape[1]
    count = pieces[0].shape[0]
    column = pl.BlockSpec((matrix.shape[0], 1, tile, tile), lambda c: (0, c + start, 0, 0))
    operands = [index, place, mask, inverse, lowers, *pieces, matrix]
    specs = [IN_SMEM] * 3 + [IN_VMEM] * (2 + len(pieces)) + [column]
    aliases = {}
    if start:
        aliases = {len(operands): 0}
        operands.append(so_far)
        specs.append(pl.BlockSpec(memory_space=pl.ANY))
    flops = 2 * count * (lowers.shape[0] * lowers.shape[1] + panels * tile * tile) * tile
    return pl.pallas_call(
        functools.partial(update_kernel, panels, skip, start),
        out_shape=jax.ShapeDtypeStruct(matrix.shape, BF16),
        grid=(count,),
        in_specs=specs,
        out_specs=column,
        scratch_shapes=[pltpu.VMEM((panels * tile, tile), BF16)],
        input_output_aliases=aliases,
        cost_estimate=pl.CostEstimate(
            flops=flops, bytes_accessed=4 * count * matrix.shape[0] * tile * tile, transcendentals=0
        ),
        compiler_params=params(),
    )(*operands)


def rows_gathered(own):
    at = lax.axis_index("prow")
    before = lax.ppermute(own, "prow", [(0, 1), (1, 2), (2, 3), (3, 0)])
    after = lax.ppermute(own, "prow", [(1, 0), (2, 1), (3, 2), (0, 3)])
    passed = jnp.where(at == 2, before, jnp.where(at == 1, after, own))
    across = lax.ppermute(passed, "prow", [(0, 2), (3, 1), (2, 3), (1, 0)])
    return [own, before, after, across]


def to_far(block):
    return lax.ppermute(block, "pcol", [(0, 4), (1, 5), (2, 6), (3, 7)])


def beside_near(block):
    return lax.ppermute(block, "pcol", [(0, 2), (2, 0), (1, 3), (3, 1)])


def beside_far(block):
    return lax.ppermute(block, "pcol", [(4, 6), (6, 4), (5, 7), (7, 5)])


def diagonal(block):
    return lax.ppermute(block, "pcol", [(0, 6), (1, 7), (2, 4), (3, 5)])


def twin(block):
    return lax.ppermute(block, "pcol", [(i, i ^ 1) for i in range(8)])


def local(small, matrix, lower_inverse, upper_inverse, row_first, col_mask):
    panels, tile = lower_inverse.shape[0], lower_inverse.shape[1]
    local_rows, local_cols = matrix.shape[0], matrix.shape[2]
    grid = matrix.reshape(local_rows, local_cols, tile, tile)
    mask = col_mask.reshape(panels, local_cols)
    row_at, column_at = lax.axis_index("prow"), lax.axis_index("pcol")
    place = jnp.stack([row_at, column_at]).astype(jnp.int32)
    skip = 1 if small else 0
    first = row_first.reshape(local_rows)[skip:]
    if small:
        cut = 2
        near = column_at < 4
        index = jnp.mod(row_at + jnp.array([0, 3, 1, 2]), 4).astype(jnp.int32)
        chunks = [rows_gathered(grid[0, :cut]), rows_gathered(grid[0, cut:])]
        half = (local_rows - 1 + 1) // 2
        col_a, col_b = grid[1 : 1 + half, 0], grid[1 + half :, 0]
        far_a, far_b = to_far(col_a), to_far(col_b)
        side_a, side_b = beside_near(col_a), beside_near(col_b)
        cross_a, cross_b = beside_far(far_a), beside_far(far_b)
        mine = jnp.stack(
            [
                jnp.where(near, jnp.concatenate([col_a, col_b]), jnp.concatenate([far_a, far_b])),
                jnp.where(near, jnp.concatenate([side_a, side_b]), jnp.concatenate([cross_a, cross_b])),
            ]
        )
        other = twin(mine)
        tops = head(panels, index, lower_inverse, chunks[0])
        heads = jnp.stack(
            [
                jnp.where(near, tops, to_far(tops)),
                jnp.where(near, beside_near(tops), diagonal(tops)),
            ]
        )
        other_heads = twin(heads)
        slot = jnp.bitwise_xor(jnp.bitwise_and(column_at, 3), jnp.array([0, 2, 1, 3])).astype(jnp.int32)
        lowers = lower(panels, slot, first, upper_inverse, [mine, other], [heads, other_heads])
    else:
        natural = jnp.arange(panels, dtype=jnp.int32)
        index = natural
        rows = lax.all_gather(grid[0], "prow")[:panels]
        chunks = [[rows[k] for k in range(panels)]]
        columns = jnp.where(natural[:, None, None, None] == column_at, grid[None, :, 0], 0)
        columns = lax.psum(columns, "pcol")
        tops = head(panels, index, lower_inverse, chunks[0])
        heads = jnp.where(natural[:, None, None, None] == column_at, tops[None], 0)
        heads = lax.psum(heads, "pcol")
        lowers = lower(panels, natural, first, upper_inverse, [columns], [heads])
    result, start = None, 0
    for pieces in chunks:
        result = update(
            panels, skip, start, index, place, mask, lower_inverse, lowers, pieces, grid, result
        )
        start += pieces[0].shape[0]
    return result.reshape(matrix.shape)


def solution(mesh):
    small = mesh.shape["prow"] == 4 and mesh.shape["pcol"] == 8

    def step(matrix, lower_inverse, upper_inverse, row_first, col_mask):
        fits = small and lower_inverse.shape[0] == 4 and matrix.shape[0] > 2 and matrix.shape[2] > 2
        return jax.shard_map(
            functools.partial(local, fits),
            mesh=mesh,
            in_specs=(
                P(None, "prow", None, "pcol", None, None),
                P(),
                P(),
                P(None, "prow"),
                P(None, None, "pcol"),
            ),
            out_specs=P(None, "prow", None, "pcol", None, None),
            check_vma=False,
        )(matrix, lower_inverse, upper_inverse, row_first, col_mask)

    return step
```

```python
import functools

import jax
import jax.numpy as jnp
from jax import lax
from jax.experimental import pallas as pl
from jax.experimental.pallas import tpu as pltpu
from jax.sharding import PartitionSpec as P

F32 = jnp.float32
BF16 = jnp.bfloat16
IN_VMEM = pl.BlockSpec(memory_space=pltpu.VMEM)
IN_SMEM = pl.BlockSpec(memory_space=pltpu.SMEM)
IN_PLACE = pl.BlockSpec(memory_space=pl.ANY)
PARAMS = pltpu.CompilerParams(vmem_limit_bytes=20 * 1024 * 1024)
SMALL = pl.CostEstimate(flops=1000, bytes_accessed=1000, transcendentals=0)
LARGE = pl.CostEstimate(flops=17_000_000_000, bytes_accessed=1000, transcendentals=0)


def near_core(array):
    return pltpu.with_memory_space_constraint(array, pltpu.VMEM)


def dot(a, b):
    return jnp.dot(a, b, preferred_element_type=F32)


def wide_dot(a, b):
    high = a.astype(BF16)
    low = (a - high.astype(F32)).astype(BF16)
    return dot(high, b) + dot(low, b)


def pick_kernel(count, index, *refs):
    pieces, out = refs[:-1], refs[-1]
    for r, piece in enumerate(pieces):

        @pl.when(index[r] < count)
        def _():
            for n in range(out.shape[0]):
                out[n, index[r]] = piece[0]


def pick(count, copies, index, pieces):
    tile = pieces[0].shape[1]
    return pl.pallas_call(
        functools.partial(pick_kernel, count),
        out_shape=pltpu.VMEM((copies, count, tile, tile), BF16),
        in_specs=[IN_SMEM] + [IN_VMEM] * len(pieces),
        out_specs=IN_VMEM,
        cost_estimate=SMALL,
        compiler_params=PARAMS,
    )(index, *map(near_core, pieces))


def choose_kernel(flag, near0, near1, far0, far1, out):
    for value, pair in ((1, (near0, near1)), (0, (far0, far1))):

        @pl.when(flag[0] == value)
        def _():
            for j, source in enumerate(pair):
                out[j] = source[...]


def choose(flag, near0, near1, far0, far1):
    return pl.pallas_call(
        choose_kernel,
        out_shape=pltpu.VMEM((2,) + near0.shape, BF16),
        in_specs=[IN_SMEM] + [IN_VMEM] * 4,
        out_specs=IN_VMEM,
        cost_estimate=SMALL,
        compiler_params=PARAMS,
    )(flag, *map(near_core, (near0, near1, far0, far1)))


def solver_kernel(panels, parts, slot, lower_inverse, upper_inverse, *refs):
    heads, out, top, wide = refs[:parts], refs[parts], refs[parts + 1], refs[parts + 2]
    tile = out.shape[0] // panels
    per = panels // parts
    for i in range(parts):
        for j in range(per):
            k = slot[i * per + j]
            for m in range(panels - 1):
                top[k, m] = heads[i][m] if per == 1 else heads[i][j, m]
    for k in range(panels):
        col = slice(k * tile, (k + 1) * tile)
        if k:
            upper = [dot(lower_inverse[m], top[k, m]).astype(BF16) for m in range(k)]
            sums = []
            for j in range(k):
                total = wide_dot(wide[j * tile : (j + 1) * tile, j * tile : (j + 1) * tile], upper[j])
                for m in range(j + 1, k):
                    total += wide_dot(wide[j * tile : (j + 1) * tile, m * tile : (m + 1) * tile], upper[m])
                sums.append(total)
            above = -wide_dot(jnp.concatenate(sums), upper_inverse[k])
            wide[: k * tile, col] = above
            out[: k * tile, col] = above.astype(BF16)
        wide[col, col] = upper_inverse[k].astype(F32)
        out[col, col] = upper_inverse[k]


def solver(panels, slot, lower_inverse, upper_inverse, heads):
    tile = lower_inverse.shape[1]
    size = panels * tile
    return pl.pallas_call(
        functools.partial(solver_kernel, panels, len(heads)),
        out_shape=pltpu.VMEM((size, size), BF16),
        in_specs=[IN_SMEM] + [IN_VMEM] * (2 + len(heads)),
        out_specs=IN_VMEM,
        scratch_shapes=[pltpu.VMEM((panels, panels - 1, tile, tile), BF16), pltpu.VMEM((size, size), F32)],
        cost_estimate=LARGE,
        compiler_params=PARAMS,
    )(slot, near_core(lower_inverse), near_core(upper_inverse), *map(near_core, heads))


def gather_kernel(panels, skip, parts, slot, first, *refs):
    columns, out = refs[:parts], refs[-1]
    tile = out.shape[1] // panels
    per = panels // parts
    for i in range(parts):
        for j in range(per):
            k = slot[i * per + j]
            across = pl.ds(pl.multiple_of(k * tile, tile), tile)
            for a in range(columns[i].shape[1]):
                live = first[skip + a, 0] <= k
                block = columns[i][j, a]
                out[a * tile : (a + 1) * tile, across] = jnp.where(live, block, jnp.zeros_like(block))


def gather(panels, skip, slot, first, columns):
    tile = columns[0].shape[2]
    return pl.pallas_call(
        functools.partial(gather_kernel, panels, skip, len(columns)),
        out_shape=pltpu.VMEM((columns[0].shape[1] * tile, panels * tile), BF16),
        in_specs=[IN_SMEM] * 2 + [IN_VMEM] * len(columns),
        out_specs=IN_VMEM,
        cost_estimate=SMALL,
        compiler_params=PARAMS,
    )(slot, first, *map(near_core, columns))


def solve_tile(index, mask, inverse, r, c, block):
    k = index[r]
    return jnp.where(mask[k, c] == 1, dot(inverse[k], block), 0.0).astype(BF16)


def band(index, r, tile):
    return pl.ds(pl.multiple_of(index[r] * tile, tile), tile)


def update_kernel(panels, skip, index, place, mask, inverse, solve, raw, held, *refs):
    pieces, out, lowers, upper, done, sem = refs[:-5], *refs[-5:]
    tile, local_rows, local_cols = held.shape[2], held.shape[0], held.shape[1]
    rows, arrays = local_rows - skip, len(pieces) // panels
    row_at, column_at = place[0], place[1]

    def copy_out(a, c):
        return pltpu.make_async_copy(done.at[a, c], out.at[a, c], sem.at[a, c])

    own = pl.ds(pl.multiple_of(jnp.minimum(row_at, panels - 1) * tile, tile), tile)
    for k in range(panels):
        lowers[:, k * tile : (k + 1) * tile] = dot(
            raw[:, : (k + 1) * tile], solve[: (k + 1) * tile, k * tile : (k + 1) * tile]
        ).astype(BF16)
    c = 0
    for n in range(arrays):
        for j in range(pieces[n].shape[0]):
            for r in range(panels):
                block = pieces[r * arrays + n][j]
                upper[c, band(index, r, tile), :] = solve_tile(index, mask, inverse, r, c, block)
            c += 1
    for c in range(local_cols):
        for a in range(rows):
            s = held[a + skip, c].astype(F32) - dot(lowers[a * tile : (a + 1) * tile, :], upper[c])
            done[a + skip, c] = s.astype(BF16)
        if c == 0:
            for k in range(panels):

                @pl.when(column_at == k)
                def _():
                    for a in range(rows):
                        done[a + skip, 0] = lowers[a * tile : (a + 1) * tile, k * tile : (k + 1) * tile]

        if skip:
            done[0, c] = upper[c, own, :]
        else:

            @pl.when(row_at < panels)
            def _():
                done[0, c] = upper[c, own, :]

        for a in range(local_rows):
            copy_out(a, c).start()
    for c in range(local_cols):
        for a in range(local_rows):
            copy_out(a, c).wait()


def update(panels, skip, index, place, mask, inverse, solve, raw, held, pieces):
    tile, rows, cols = held.shape[2], held.shape[0], held.shape[1]
    flat = [array for piece in pieces for array in piece]
    return pl.pallas_call(
        functools.partial(update_kernel, panels, skip),
        out_shape=jax.ShapeDtypeStruct(held.shape, BF16),
        in_specs=[IN_SMEM] * 3 + [IN_VMEM] * (4 + len(flat)),
        out_specs=IN_PLACE,
        scratch_shapes=[
            pltpu.VMEM(raw.shape, BF16),
            pltpu.VMEM((cols, panels * tile, tile), BF16),
            pltpu.VMEM(held.shape, BF16),
            pltpu.SemaphoreType.DMA((rows, cols)),
        ],
        cost_estimate=SMALL,
        compiler_params=PARAMS,
    )(index, place, mask, near_core(inverse), solve, raw, held, *map(near_core, flat))


def along_rows(block, pairs):
    return lax.ppermute(block, "prow", pairs)


def up(block):
    return along_rows(block, [(0, 1), (1, 2), (2, 3), (3, 0)])


def down(block):
    return along_rows(block, [(1, 0), (2, 1), (3, 2), (0, 3)])


def over(block):
    return along_rows(block, [(0, 2), (1, 3), (2, 0), (3, 1)])


def to_far(block):
    return lax.ppermute(block, "pcol", [(0, 4), (1, 5), (2, 6), (3, 7)])


def beside_near(block):
    return lax.ppermute(block, "pcol", [(0, 2), (2, 0), (1, 3), (3, 1)])


def beside_far(block):
    return lax.ppermute(block, "pcol", [(4, 6), (6, 4), (5, 7), (7, 5)])


def twin(block):
    return lax.ppermute(block, "pcol", [(i, i ^ 1) for i in range(8)])


def after(block, *others):
    return lax.optimization_barrier((block, *others))[0]


def local(small, matrix, lower_inverse, upper_inverse, row_first, col_mask):
    panels, tile = lower_inverse.shape[0], lower_inverse.shape[1]
    local_rows, local_cols = matrix.shape[0], matrix.shape[2]
    grid = matrix.reshape(local_rows, local_cols, tile, tile)
    mask = col_mask.reshape(panels, local_cols)
    row_at, column_at = lax.axis_index("prow"), lax.axis_index("pcol")
    place = jnp.stack([row_at, column_at]).astype(jnp.int32)
    natural = jnp.arange(panels, dtype=jnp.int32)
    if small:
        skip = 1
        near = (column_at < 4).astype(jnp.int32).reshape(1)
        index = jnp.mod(row_at + jnp.array([0, 3, 1, 2]), 4).astype(jnp.int32)
        slot = jnp.bitwise_xor(jnp.bitwise_and(column_at, 3), jnp.array([0, 2, 1, 3])).astype(jnp.int32)
        own0, own1, column = grid[0, :1], grid[0, 1:], grid[1:, 0]

        up0, down0, over0 = up(own0), down(own0), over(own0)
        far = to_far(column)
        own1 = after(own1, up0, down0, over0)
        up1, down1 = up(own1), down(own1)
        side = beside_near(after(column, up0, down0, over0))
        cross = beside_far(far)
        tops = pick(panels - 1, 4, index, [own0, up0, down0, over0])
        tops = lax.all_to_all(tops, "pcol", 0, 0, axis_index_groups=[[0, 2, 4, 6], [1, 3, 5, 7]], tiled=True)

        passed = jnp.where(row_at == 2, up1, jnp.where(row_at == 1, down1, own1))
        rest = along_rows(passed, [(0, 2), (3, 1), (2, 3), (1, 0)])
        heads = [tops[0], tops[1]]
        core = jnp.bitwise_and(column_at, 1)
        head_slot = jnp.bitwise_xor(core, jnp.array([0, 2, 1, 3])).astype(jnp.int32)
        solve = solver(panels, head_slot, lower_inverse, upper_inverse, [after(heads[0], rest), heads[1], twin(heads[0]), twin(heads[1])])
        mine = choose(near, column, side, far, after(cross, passed))
        columns = [mine, twin(mine)]
        pieces = [[own0, own1], [up0, up1], [down0, down1], [over0, rest]]
    else:
        skip, index, slot = 0, natural, natural
        rows = lax.all_gather(grid[0], "prow")[:panels]
        pieces = [[rows[k]] for k in range(panels)]
        columns = jnp.where(natural[:, None, None, None] == column_at, grid[None, :, 0], 0)
        columns = [lax.psum(columns, "pcol")]
        tops = pick(panels - 1, 1, index, [rows[k] for k in range(panels)])[0]
        heads = jnp.where(natural[:, None, None, None] == column_at, tops[None], 0)
        heads = lax.psum(heads, "pcol")
        solve = solver(panels, natural, lower_inverse, upper_inverse, [heads])
    held = pltpu.with_memory_space_constraint(grid, pltpu.VMEM)
    raw = gather(panels, skip, slot, row_first, columns)
    result = update(panels, skip, index, place, mask, lower_inverse, solve, raw, held, pieces)
    return result.reshape(matrix.shape)


def solution(mesh):
    small = mesh.shape["prow"] == 4 and mesh.shape["pcol"] == 8

    def step(matrix, lower_inverse, upper_inverse, row_first, col_mask):
        fits = small and lower_inverse.shape[0] == 4 and matrix.shape[0] > 2 and matrix.shape[2] > 2
        return jax.shard_map(
            functools.partial(local, fits),
            mesh=mesh,
            in_specs=(
                P(None, "prow", None, "pcol", None, None),
                P(),
                P(),
                P(None, "prow"),
                P(None, None, "pcol"),
            ),
            out_specs=P(None, "prow", None, "pcol", None, None),
            check_vma=False,
        )(matrix, lower_inverse, upper_inverse, row_first, col_mask)

    return step
```

```python
import functools

import jax
import jax.numpy as jnp
from jax import lax
from jax.experimental import pallas as pl
from jax.experimental.pallas import tpu as pltpu
from jax.sharding import PartitionSpec as P

F32 = jnp.float32
BF16 = jnp.bfloat16
IN_VMEM = pl.BlockSpec(memory_space=pltpu.VMEM)
IN_SMEM = pl.BlockSpec(memory_space=pltpu.SMEM)
IN_PLACE = pl.BlockSpec(memory_space=pl.ANY)
PARAMS = pltpu.CompilerParams(vmem_limit_bytes=20 * 1024 * 1024)
SMALL = pl.CostEstimate(flops=1000, bytes_accessed=1000, transcendentals=0)
LARGE = pl.CostEstimate(flops=17_000_000_000, bytes_accessed=1000, transcendentals=0)


def near_core(array):
    return pltpu.with_memory_space_constraint(array, pltpu.VMEM)


def dot(a, b):
    return jnp.dot(a, b, preferred_element_type=F32)


def wide_dot(a, b):
    high = a.astype(BF16)
    low = (a - high.astype(F32)).astype(BF16)
    return dot(high, b) + dot(low, b)


def pick_kernel(count, index, *refs):
    pieces, out = refs[:-1], refs[-1]
    for r, piece in enumerate(pieces):

        @pl.when(index[r] < count)
        def _():
            for n in range(out.shape[0]):
                out[n, index[r]] = piece[0]


def pick(count, copies, index, pieces):
    tile = pieces[0].shape[1]
    return pl.pallas_call(
        functools.partial(pick_kernel, count),
        out_shape=pltpu.VMEM((copies, count, tile, tile), BF16),
        in_specs=[IN_SMEM] + [IN_VMEM] * len(pieces),
        out_specs=IN_VMEM,
        cost_estimate=SMALL,
        compiler_params=PARAMS,
    )(index, *map(near_core, pieces))


def choose_kernel(flag, near0, near1, far0, far1, out):
    for value, pair in ((1, (near0, near1)), (0, (far0, far1))):

        @pl.when(flag[0] == value)
        def _():
            for j, source in enumerate(pair):
                out[j] = source[...]


def choose(flag, near0, near1, far0, far1):
    return pl.pallas_call(
        choose_kernel,
        out_shape=pltpu.VMEM((2,) + near0.shape, BF16),
        in_specs=[IN_SMEM] + [IN_VMEM] * 4,
        out_specs=IN_VMEM,
        cost_estimate=SMALL,
        compiler_params=PARAMS,
    )(flag, *map(near_core, (near0, near1, far0, far1)))


def solver_kernel(panels, parts, slot, lower_inverse, upper_inverse, *refs):
    heads, out, top, wide = refs[:parts], refs[parts], refs[parts + 1], refs[parts + 2]
    tile = out.shape[0] // panels
    per = panels // parts
    for i in range(parts):
        for j in range(per):
            k = slot[i * per + j]
            for m in range(panels - 1):
                top[k, m] = heads[i][m] if per == 1 else heads[i][j, m]
    for k in range(panels):
        col = slice(k * tile, (k + 1) * tile)
        if k:
            upper = [dot(lower_inverse[m], top[k, m]).astype(BF16) for m in range(k)]
            sums = []
            for j in range(k):
                total = wide_dot(wide[j * tile : (j + 1) * tile, j * tile : (j + 1) * tile], upper[j])
                for m in range(j + 1, k):
                    total += wide_dot(wide[j * tile : (j + 1) * tile, m * tile : (m + 1) * tile], upper[m])
                sums.append(total)
            above = -wide_dot(jnp.concatenate(sums), upper_inverse[k])
            wide[: k * tile, col] = above
            out[: k * tile, col] = above.astype(BF16)
        wide[col, col] = upper_inverse[k].astype(F32)
        out[col, col] = upper_inverse[k]


def solver(panels, slot, lower_inverse, upper_inverse, heads):
    tile = lower_inverse.shape[1]
    size = panels * tile
    return pl.pallas_call(
        functools.partial(solver_kernel, panels, len(heads)),
        out_shape=pltpu.VMEM((size, size), BF16),
        in_specs=[IN_SMEM] + [IN_VMEM] * (2 + len(heads)),
        out_specs=IN_VMEM,
        scratch_shapes=[pltpu.VMEM((panels, panels - 1, tile, tile), BF16), pltpu.VMEM((size, size), F32)],
        cost_estimate=LARGE,
        compiler_params=PARAMS,
    )(slot, near_core(lower_inverse), near_core(upper_inverse), *map(near_core, heads))


def gather_kernel(panels, skip, parts, slot, first, *refs):
    columns, out = refs[:parts], refs[-1]
    tile = out.shape[1] // panels
    per = panels // parts
    for i in range(parts):
        for j in range(per):
            k = slot[i * per + j]
            across = pl.ds(pl.multiple_of(k * tile, tile), tile)
            for a in range(columns[i].shape[1]):
                live = first[skip + a, 0] <= k
                block = columns[i][j, a]
                out[a * tile : (a + 1) * tile, across] = jnp.where(live, block, jnp.zeros_like(block))


def gather(panels, skip, slot, first, columns):
    tile = columns[0].shape[2]
    return pl.pallas_call(
        functools.partial(gather_kernel, panels, skip, len(columns)),
        out_shape=pltpu.VMEM((columns[0].shape[1] * tile, panels * tile), BF16),
        in_specs=[IN_SMEM] * 2 + [IN_VMEM] * len(columns),
        out_specs=IN_VMEM,
        cost_estimate=SMALL,
        compiler_params=PARAMS,
    )(slot, first, *map(near_core, columns))


def solve_tile(index, mask, inverse, r, c, block):
    k = index[r]
    return jnp.where(mask[k, c] == 1, dot(inverse[k], block), 0.0).astype(BF16)


def band(index, r, tile):
    return pl.ds(pl.multiple_of(index[r] * tile, tile), tile)


def update_kernel(panels, skip, index, place, mask, inverse, solve, raw, held, *refs):
    pieces, out, lowers, upper, done, sem = refs[:-5], *refs[-5:]
    tile, local_rows, local_cols = held.shape[2], held.shape[0], held.shape[1]
    rows, arrays = local_rows - skip, len(pieces) // panels
    row_at, column_at = place[0], place[1]

    def copy_out(a, c):
        return pltpu.make_async_copy(done.at[a, c], out.at[a, c], sem.at[a, c])

    own = pl.ds(pl.multiple_of(jnp.minimum(row_at, panels - 1) * tile, tile), tile)
    for k in range(panels):
        lowers[:, k * tile : (k + 1) * tile] = dot(
            raw[:, : (k + 1) * tile], solve[: (k + 1) * tile, k * tile : (k + 1) * tile]
        ).astype(BF16)
    c = 0
    for n in range(arrays):
        for j in range(pieces[n].shape[0]):
            for r in range(panels):
                block = pieces[r * arrays + n][j]
                upper[c, band(index, r, tile), :] = solve_tile(index, mask, inverse, r, c, block)
            c += 1
    for c in range(local_cols):
        for a in range(rows):
            s = held[a + skip, c].astype(F32) - dot(lowers[a * tile : (a + 1) * tile, :], upper[c])
            done[a + skip, c] = s.astype(BF16)
        if c == 0:
            for k in range(panels):

                @pl.when(column_at == k)
                def _():
                    for a in range(rows):
                        done[a + skip, 0] = lowers[a * tile : (a + 1) * tile, k * tile : (k + 1) * tile]

        if skip:
            done[0, c] = upper[c, own, :]
        else:

            @pl.when(row_at < panels)
            def _():
                done[0, c] = upper[c, own, :]

        for a in range(local_rows):
            copy_out(a, c).start()
    for c in range(local_cols):
        for a in range(local_rows):
            copy_out(a, c).wait()


def update(panels, skip, index, place, mask, inverse, solve, raw, held, pieces):
    tile, rows, cols = held.shape[2], held.shape[0], held.shape[1]
    flat = [array for piece in pieces for array in piece]
    return pl.pallas_call(
        functools.partial(update_kernel, panels, skip),
        out_shape=jax.ShapeDtypeStruct(held.shape, BF16),
        in_specs=[IN_SMEM] * 3 + [IN_VMEM] * (4 + len(flat)),
        out_specs=IN_PLACE,
        scratch_shapes=[
            pltpu.VMEM(raw.shape, BF16),
            pltpu.VMEM((cols, panels * tile, tile), BF16),
            pltpu.VMEM(held.shape, BF16),
            pltpu.SemaphoreType.DMA((rows, cols)),
        ],
        cost_estimate=SMALL,
        compiler_params=PARAMS,
    )(index, place, mask, near_core(inverse), solve, raw, held, *map(near_core, flat))


def along_rows(block, pairs):
    return lax.ppermute(block, "prow", pairs)


def up(block):
    return along_rows(block, [(0, 1), (1, 2), (2, 3), (3, 0)])


def down(block):
    return along_rows(block, [(1, 0), (2, 1), (3, 2), (0, 3)])


def over(block):
    return along_rows(block, [(0, 2), (1, 3), (2, 0), (3, 1)])


def to_far(block):
    return lax.ppermute(block, "pcol", [(0, 4), (1, 5), (2, 6), (3, 7)])


def beside_near(block):
    return lax.ppermute(block, "pcol", [(0, 2), (2, 0), (1, 3), (3, 1)])


def beside_far(block):
    return lax.ppermute(block, "pcol", [(4, 6), (6, 4), (5, 7), (7, 5)])


def twin(block):
    return lax.ppermute(block, "pcol", [(i, i ^ 1) for i in range(8)])


def after(block, *others):
    return lax.optimization_barrier((block, *others))[0]


def local(small, matrix, lower_inverse, upper_inverse, row_first, col_mask):
    panels, tile = lower_inverse.shape[0], lower_inverse.shape[1]
    local_rows, local_cols = matrix.shape[0], matrix.shape[2]
    grid = matrix.reshape(local_rows, local_cols, tile, tile)
    mask = col_mask.reshape(panels, local_cols)
    row_at, column_at = lax.axis_index("prow"), lax.axis_index("pcol")
    place = jnp.stack([row_at, column_at]).astype(jnp.int32)
    natural = jnp.arange(panels, dtype=jnp.int32)
    if small:
        skip = 1
        near = (column_at < 4).astype(jnp.int32).reshape(1)
        index = jnp.mod(row_at + jnp.array([0, 3, 1, 2]), 4).astype(jnp.int32)
        slot = jnp.bitwise_xor(jnp.bitwise_and(column_at, 3), jnp.array([0, 2, 1, 3])).astype(jnp.int32)
        own0, own1, column = grid[0, :1], grid[0, 1:], grid[1:, 0]

        up0, down0, over0 = up(own0), down(own0), over(own0)
        far = to_far(column)
        own1 = after(own1, up0, down0, over0)
        up1, down1 = up(own1), down(own1)
        side = beside_near(after(column, up0, down0, over0))
        cross = beside_far(far)
        tops = pick(panels - 1, 4, index, [own0, up0, down0, over0])
        tops = lax.all_to_all(tops, "pcol", 0, 0, axis_index_groups=[[0, 2, 4, 6], [1, 3, 5, 7]], tiled=True)

        passed = jnp.where(row_at == 2, up1, jnp.where(row_at == 1, down1, own1))
        rest = along_rows(passed, [(0, 2), (3, 1), (2, 3), (1, 0)])
        heads = [tops[0], tops[1]]
        core = jnp.bitwise_and(column_at, 1)
        head_slot = jnp.bitwise_xor(core, jnp.array([0, 2, 1, 3])).astype(jnp.int32)
        solve = solver(panels, head_slot, lower_inverse, upper_inverse, [after(heads[0], rest), heads[1], twin(heads[0]), twin(heads[1])])
        mine = choose(near, column, side, far, cross)
        columns = [mine, twin(mine)]
        pieces = [[own0, own1], [up0, up1], [down0, down1], [over0, rest]]
    else:
        skip, index, slot = 0, natural, natural
        rows = lax.all_gather(grid[0], "prow")[:panels]
        pieces = [[rows[k]] for k in range(panels)]
        columns = jnp.where(natural[:, None, None, None] == column_at, grid[None, :, 0], 0)
        columns = [lax.psum(columns, "pcol")]
        tops = pick(panels - 1, 1, index, [rows[k] for k in range(panels)])[0]
        heads = jnp.where(natural[:, None, None, None] == column_at, tops[None], 0)
        heads = lax.psum(heads, "pcol")
        solve = solver(panels, natural, lower_inverse, upper_inverse, [heads])
    held = pltpu.with_memory_space_constraint(grid, pltpu.VMEM)
    raw = gather(panels, skip, slot, row_first, columns)
    result = update(panels, skip, index, place, mask, lower_inverse, solve, raw, held, pieces)
    return result.reshape(matrix.shape)


def solution(mesh):
    small = mesh.shape["prow"] == 4 and mesh.shape["pcol"] == 8

    def step(matrix, lower_inverse, upper_inverse, row_first, col_mask):
        fits = small and lower_inverse.shape[0] == 4 and matrix.shape[0] > 2 and matrix.shape[2] > 2
        return jax.shard_map(
            functools.partial(local, fits),
            mesh=mesh,
            in_specs=(
                P(None, "prow", None, "pcol", None, None),
                P(),
                P(),
                P(None, "prow"),
                P(None, None, "pcol"),
            ),
            out_specs=P(None, "prow", None, "pcol", None, None),
            check_vma=False,
        )(matrix, lower_inverse, upper_inverse, row_first, col_mask)

    return step
```
